32 devices in a mesh: leaf: 8 (over z, y), rhs: 4 (over x, core).
Axes of the slice: x: 2, y: 2, z: 4, core: 2. Of those that a mesh axis runs over, the one named last changes fastest.
Arguments:
- points: bfloat16 [64, 65536], P('rhs', 'leaf'), may hold values from -6 to 6
- leaf_basis: bfloat16 [256, 64, 256], P('leaf'), may hold values from -0.375 to 0.375
- local_transfer: bfloat16 [8, 31, 64, 128], P('leaf'), may hold values from -0.625 to 0.625
- top_transfer: bfloat16 [6, 64, 128], replicated, may hold values from -0.625 to 0.625
- leaf_coupling: bfloat16 [3, 256, 64, 320], P(None, 'leaf'), may hold values from -0.3125 to 0.3125
- root_coupling: bfloat16 [3, 8, 64, 192], P(None, 'leaf'), may hold values from -0.4375 to 0.4375
- upper_coupling: bfloat16 [3, 6, 64, 192], replicated, may hold values from -0.4375 to 0.4375
- near_blocks: bfloat16 [3, 256, 3, 256, 256], P(None, 'leaf', None, 'rhs'), may hold values from -0.21875 to 0.21875
- near_offset: int32 [256, 3], P('leaf'), may hold values from -8 to 8, as said below
- far_offset: int32 [256, 5], P('leaf'), may hold values from -8 to 8, as said below
Outputs:
- applied: bfloat16 [3, 64, 65536], P(None, 'rhs', 'leaf')
The draws below stay inside these ranges and needn't reach their ends.
Inputs may be any that keep to these rules, and one draw needn't show every extreme that they name: `near_offset`: the first entry of each row is 0; the entries of a row are distinct and lie within 8 of 0. `far_offset`: entries are nonzero, distinct within a row, and differ from every entry of the same row of near_offset.
All inputs are finite; a program needn't handle non-finite values.
Results may differ from the reference program's by a relative error of at most 0.025.
Values may be sent and summed in bfloat16 or wider, within the bound.
A program may use at most 192 MiB of HBM per device.

```python
import jax
import jax.numpy as jnp
from jax import lax

LEAF = 256
RANK = 64
NCOL = 64
OPS = 3
LPD = 32
W = 8
NEAR = 3
FAR = 5
TOPL = 3
NLEAF = 256
NPTS = 65536
SUP = 6
N_LEAF = 8


def window_shuffle(key):
    leaf_keys = jax.random.split(key, NLEAF)
    candidates = jnp.concatenate([jnp.arange(-W, 0, dtype=jnp.int32), jnp.arange(1, W + 1, dtype=jnp.int32)])
    return jax.vmap(lambda single: jax.random.permutation(single, candidates))(leaf_keys).astype(jnp.int32)


def draw_near_offset(key, part):
    shuffled = window_shuffle(key)
    self_column = jnp.zeros((NLEAF, 1), dtype=jnp.int32)
    return jnp.concatenate([self_column, shuffled[:, :NEAR - 1]], axis=1)


def draw_far_offset(key, part):
    shuffled = window_shuffle(key)
    return shuffled[:, NEAR - 1:NEAR - 1 + FAR]


def steps_of(stream_key, shape, pieces, low, largest):
    loudness = 1.0
    for dim, blocks in pieces:
        heights = jax.random.uniform(jax.random.fold_in(jax.random.fold_in(stream_key, 6), dim), (blocks,), jnp.float32, low / len(pieces), largest / len(pieces))
        loudness = loudness * jnp.repeat(jnp.exp(heights), shape[dim] // blocks).reshape((-1,) + (1,) * (len(shape) - 1 - dim))
    return loudness


def normal_values(stream_key, extent, scale, reach, cuts=(), kind=jnp.bfloat16):
    values = scale * jax.random.normal(stream_key, extent, jnp.float32)
    if cuts:
        values = values * steps_of(stream_key, extent, cuts, -0.22, 0.18)
    return jnp.clip(values, -reach, reach).astype(kind)


def setup_inputs(seed: int = 0) -> dict:
    streams_of = jax.random.split(jax.random.key(seed), 11)
    return {
        "points": normal_values(streams_of[0], (NCOL, NPTS), 1.0, 6.0, ((0, 4), (1, 8))),
        "leaf_basis": normal_values(streams_of[1], (NLEAF, RANK, LEAF), LEAF ** -0.5, 0.375, ((0, 8),)),
        "local_transfer": normal_values(streams_of[2], (N_LEAF, LPD - 1, RANK, 2 * RANK), (3 * RANK // 2) ** -0.5, 0.625, ((0, 8),)),
        "top_transfer": normal_values(streams_of[3], (SUP, RANK, 2 * RANK), (3 * RANK // 2) ** -0.5, 0.625),
        "leaf_coupling": normal_values(streams_of[4], (OPS, NLEAF, RANK, FAR * RANK), (FAR * RANK) ** -0.5, 0.3125, ((1, 8),)),
        "root_coupling": normal_values(streams_of[5], (OPS, N_LEAF, RANK, 3 * RANK), (3 * RANK) ** -0.5, 0.4375, ((1, 8),)),
        "upper_coupling": normal_values(streams_of[6], (OPS, SUP, RANK, 3 * RANK), (3 * RANK) ** -0.5, 0.4375),
        "near_blocks": normal_values(streams_of[7], (OPS, NLEAF, NEAR, LEAF, LEAF), (NEAR * LEAF) ** -0.5, 0.21875, ((1, 8), (3, 4))),
        "near_offset": draw_near_offset(jax.random.fold_in(streams_of[10], 71), 0),
        "far_offset": draw_far_offset(jax.random.fold_in(streams_of[10], 71), 0),
    }


def round_half(values):
    return lax.optimization_barrier(values.astype(jnp.bfloat16))


def pair_up(level_coef, transfer):
    col_count, cluster_count, rank_size = level_coef.shape
    joined = level_coef.reshape(col_count, cluster_count // 2, 2 * rank_size).astype(jnp.float32)
    return round_half(jnp.einsum('cpk,prk->cpr', joined, transfer.astype(jnp.float32)))


def pair_down(field, transfer):
    ops_count, col_count, cluster_count, rank_size = field.shape
    narrow = round_half(field).astype(jnp.float32)
    children = jnp.einsum('ocpr,prk->ocpk', narrow, transfer.astype(jnp.float32))
    return children.reshape(ops_count, col_count, 2 * cluster_count, rank_size)


def cousin_sources(level_coef):
    col_count, cluster_count, rank_size = level_coef.shape
    padded = jnp.pad(level_coef, ((0, 0), (3, 3), (0, 0)))
    clusters = jnp.arange(cluster_count, dtype=jnp.int32)[:, None]
    steps_even = jnp.array([-2, 2, 3], dtype=jnp.int32)[None, :]
    steps_odd = jnp.array([-3, -2, 2], dtype=jnp.int32)[None, :]
    chosen = jnp.where(clusters % 2 == 0, steps_even, steps_odd)
    rows_taken = (3 + clusters + chosen).astype(jnp.int32)
    picked = jnp.take(padded, rows_taken.reshape(-1), axis=1)
    return picked.reshape(col_count, cluster_count, 3 * rank_size)


def reference(points, leaf_basis, local_transfer, top_transfer, leaf_coupling, root_coupling, upper_coupling, near_blocks, near_offset, far_offset):
    col_count = points.shape[0]
    leaf_count = leaf_basis.shape[0]
    leaf_points = points.reshape(col_count, leaf_count, LEAF)
    leaf_coef = round_half(jnp.einsum('cti,tri->ctr', leaf_points.astype(jnp.float32), leaf_basis.astype(jnp.float32)))
    depth_local = LPD.bit_length() - 1
    transfers = []
    current = leaf_coef
    offset = 0
    for height in range(depth_local):
        cluster_count = LPD >> (height + 1)
        transfer = local_transfer[:, offset:offset + cluster_count].reshape(N_LEAF * cluster_count, RANK, 2 * RANK)
        transfers.append(transfer)
        current = pair_up(current, transfer)
        offset += cluster_count
    level_coef = current
    fields = []
    for height in range(TOPL):
        level_size = N_LEAF >> height
        if height == 0:
            coupling = root_coupling
        else:
            first_row = N_LEAF - N_LEAF // 2 ** (height - 1)
            level_coef = pair_up(level_coef, top_transfer[first_row:first_row + level_size])
            coupling = upper_coupling[:, first_row:first_row + level_size]
        sources = cousin_sources(level_coef).astype(jnp.float32)
        fields.append(jnp.einsum('cmk,omrk->ocmr', sources, coupling.astype(jnp.float32)))
    running = fields[TOPL - 1]
    for height in range(TOPL - 1, 0, -1):
        first_row = N_LEAF - N_LEAF // 2 ** (height - 1)
        running = fields[height - 1] + pair_down(running, top_transfer[first_row:first_row + (N_LEAF >> height)])
    for height in reversed(range(depth_local)):
        running = pair_down(running, transfers[height])
    leaf_range = jnp.arange(leaf_count, dtype=jnp.int32)[:, None]
    wide_coef = jnp.pad(leaf_coef, ((0, 0), (W, W), (0, 0)))
    far_index = (W + leaf_range + far_offset).astype(jnp.int32)
    sources = jnp.take(wide_coef, far_index.reshape(-1), axis=1).reshape(col_count, leaf_count, FAR * RANK).astype(jnp.float32)
    coupled = jnp.einsum('ctk,otrk->octr', sources, leaf_coupling.astype(jnp.float32))
    leaf_field = round_half(running + coupled).astype(jnp.float32)
    far_part = jnp.einsum('octr,tri->octi', leaf_field, leaf_basis.astype(jnp.float32))
    wide_points = jnp.pad(leaf_points, ((0, 0), (W, W), (0, 0)))
    near_index = (W + leaf_range + near_offset).astype(jnp.int32)

    def group_near(group):
        start_leaf = (group * LPD).astype(jnp.int32)
        wanted = lax.dynamic_slice_in_dim(near_index, start_leaf, LPD, 0)
        local_sources = jnp.take(wide_points, wanted.reshape(-1), axis=1).reshape(col_count, LPD, NEAR, LEAF).astype(jnp.float32)
        blocks = lax.dynamic_slice_in_dim(near_blocks, start_leaf, LPD, 1).astype(jnp.float32)
        return jnp.einsum('ctkj,otkij->octi', local_sources, blocks)

    grouped = lax.map(group_near, jnp.arange(N_LEAF, dtype=jnp.int32))
    near_part = jnp.transpose(grouped, (1, 2, 0, 3, 4)).reshape(OPS, col_count, leaf_count, LEAF)
    return (far_part + near_part).astype(jnp.bfloat16).reshape(OPS, col_count, leaf_count * LEAF)
```

```python
import functools

import jax
import jax.numpy as jnp
from jax import lax
from jax.experimental import pallas as pl
from jax.experimental.pallas import tpu as pltpu
from jax.sharding import PartitionSpec as P

LEAF = 256
OPS = 3
W = 8
NEAR = 3
FAR = 5
TOPL = 3
RHS = 4
CHUNKS = 4
UNROLL = 4
MESH = pl.DeviceIdType.MESH
F32 = jnp.float32
BF16 = jnp.bfloat16


def dot_nt(a, b):
    return lax.dot_general(a, b, (((1,), (1,)), ((), ())), preferred_element_type=F32)


def dot_nn(a, b):
    return lax.dot_general(a, b, (((1,), (0,)), ((), ())), preferred_element_type=F32)


def twice(values):
    return jnp.concatenate([values, values], axis=-1).astype(BF16)


def kernel(
    groups,
    points,
    near_offset,
    far_offset,
    basis_hbm,
    local_hbm,
    top_hbm,
    coupling_hbm,
    root_hbm,
    upper_hbm,
    blocks_hbm,
    out,
    basis,
    local,
    top,
    coupling,
    root_k,
    upper_k,
    blocks,
    wide,
    coef,
    level_coef,
    roots,
    upper_coef,
    coupled,
    fields,
    near_send,
    near_recv,
    in_sem,
    send_sem,
    recv_sem,
    root_send,
    root_recv,
    near_ssem,
    near_rsem,
):
    cols = points.shape[0]
    leaves = basis.shape[0]
    rank = basis.shape[1]
    pairs = leaves // 2
    me_l = lax.axis_index("leaf")
    me_r = lax.axis_index("rhs")
    side = me_r + 1 - 2 * (me_r % 2)
    across = (me_r + 2) % 4
    diagonal = (side + 2) % 4
    peers = (me_r, side, across, diagonal)
    has_left = me_l > 0
    has_right = me_l < groups - 1
    top_w = W + leaves

    loads = [
        pltpu.make_async_copy(source, target, in_sem.at[i])
        for i, (source, target) in enumerate(
            [
                (basis_hbm, basis),
                (local_hbm, local),
                (coupling_hbm, coupling),
                (blocks_hbm, blocks),
                (top_hbm, top),
                (root_hbm, root_k),
                (upper_hbm, upper_k),
            ]
        )
    ]
    for load in loads:
        load.start()

    barrier = pltpu.get_barrier_semaphore()
    for peer in peers[1:]:
        pl.semaphore_signal(barrier, inc=1, device_id=(me_l, peer), device_id_type=MESH)
    for step in range(1, groups):
        pl.semaphore_signal(
            barrier, inc=1, device_id=((me_l + step) % groups, me_r), device_id_type=MESH
        )

    for t in range(leaves):
        wide[0, W + t] = points[:, t * LEAF : (t + 1) * LEAF]
    low, high = pl.ds(0, W), pl.ds(top_w, W)
    head, tail = pl.ds(W, W), pl.ds(leaves, W)
    middle = pl.ds(2 * W, leaves - 2 * W)
    body = pl.ds(W, leaves)

    @pl.when(jnp.logical_not(has_left))
    def _():
        wide[:, 0:W] = jnp.zeros((RHS, W, cols, LEAF), BF16)
        coef[0:W] = jnp.zeros((W, cols, 2 * rank), BF16)

    @pl.when(jnp.logical_not(has_right))
    def _():
        wide[:, top_w : top_w + W] = jnp.zeros((RHS, W, cols, LEAF), BF16)
        coef[top_w : top_w + W] = jnp.zeros((W, cols, 2 * rank), BF16)

    roots[0:3] = jnp.zeros((3, cols, 2 * rank), BF16)
    roots[3 + groups : 6 + groups] = jnp.zeros((3, cols, 2 * rank), BF16)
    upper_coef[...] = jnp.zeros(upper_coef.shape, BF16)

    right = (me_l + 1) % groups
    left = (me_l + groups - 1) % groups

    def remote(number, source, target, leaf, rhs):
        return pltpu.make_async_remote_copy(
            src_ref=source,
            dst_ref=target,
            send_sem=send_sem.at[number],
            recv_sem=recv_sem.at[number],
            device_id=(leaf, rhs),
            device_id_type=MESH,
        )

    def part(slot, where):
        return wide.at[slot, where]

    copies = {
        0: (part(0, head), part(2, head), me_l, across),
        1: (part(0, tail), part(2, tail), me_l, across),
        2: (part(0, middle), part(2, middle), me_l, across),
        3: (part(0, body), part(1, body), me_l, side),
        4: (part(0, tail), part(0, low), right, me_r),
        5: (part(0, head), part(0, high), left, me_r),
        6: (part(2, tail), part(2, low), right, me_r),
        7: (part(2, head), part(2, high), left, me_r),
        8: (part(2, head), part(3, head), me_l, side),
        9: (part(2, tail), part(3, tail), me_l, side),
        10: (part(2, middle), part(3, middle), me_l, side),
        11: (part(0, low), part(1, low), me_l, side),
        12: (part(0, high), part(1, high), me_l, side),
        13: (part(2, low), part(3, low), me_l, side),
        14: (part(2, high), part(3, high), me_l, side),
        15: (coef.at[tail], coef.at[low], right, me_r),
        16: (coef.at[head], coef.at[high], left, me_r),
    }
    to_right = (4, 6, 15)
    to_left = (5, 7, 16)
    from_low = (11, 13)
    from_high = (12, 14)

    def guard(number, receiving):
        if number in to_right:
            return has_left if receiving else has_right
        if number in to_left:
            return has_right if receiving else has_left
        if number in from_low:
            return has_left
        if number in from_high:
            return has_right
        return None

    def run(number, action):
        condition = guard(number, action == "wait_recv")

        def go():
            getattr(remote(number, *copies[number]), action)()

        if condition is None:
            go()
        else:
            pl.when(condition)(go)

    def start(number):
        run(number, "start")

    def arrived(number):
        run(number, "wait_recv")

    pl.semaphore_wait(barrier, len(peers) - 1 + groups - 1)
    for number in (0, 1, 4, 5, 2, 3):
        start(number)

    first_half = lax.broadcasted_iota(jnp.int32, (cols, 2 * rank), 1) < rank

    def joined(a, b):
        return jnp.where(first_half, a.astype(F32), b.astype(F32)).astype(BF16)

    loads[0].wait()

    @pl.loop(0, leaves // UNROLL)
    def _(step):
        for u in range(UNROLL):
            t = step * UNROLL + u
            coef[W + t] = twice(dot_nt(wide[0, W + t], basis[t]))

    start(15)
    start(16)

    arrived(0)
    start(7)
    start(8)
    arrived(1)
    start(6)
    start(9)

    loads[1].wait()
    depth = leaves.bit_length() - 1
    offset = 0
    base = 0
    for height in range(depth):
        count = leaves >> height + 1
        for p in range(count):
            if height == 0:
                pair = joined(coef[W + 2 * p], coef[W + 2 * p + 1])
            else:
                pair = joined(level_coef[base + 2 * p], level_coef[base + 2 * p + 1])
            level_coef[offset + p] = twice(dot_nt(pair, local[0, offset + p]))
        base = offset
        offset += count
    roots[3 + me_l] = level_coef[leaves - 2]

    def root_copy(step):
        return pltpu.make_async_remote_copy(
            src_ref=roots.at[3 + me_l],
            dst_ref=roots.at[3 + me_l],
            send_sem=root_send.at[step - 1],
            recv_sem=root_recv.at[step - 1],
            device_id=((me_l + step) % groups, me_r),
            device_id_type=MESH,
        )

    for step in range(1, groups):
        root_copy(step).start()

    arrived(4)
    start(11)
    arrived(5)
    start(12)
    arrived(15)
    arrived(16)

    loads[2].wait()

    @pl.loop(0, leaves // UNROLL)
    def _(step):
        for u in range(UNROLL):
            t = step * UNROLL + u
            picked = [coef[W + t + far_offset[t, k]] for k in range(FAR)]
            pieces = [joined(picked[k], picked[k + 1]) for k in range(0, FAR - 1, 2)]
            pieces.append(picked[FAR - 1][:, :rank])
            sources = jnp.concatenate(pieces, axis=-1)
            for o in range(OPS):
                coupled[t, o * cols : (o + 1) * cols] = dot_nt(sources, coupling[o, t])

    arrived(6)
    start(13)
    arrived(7)
    start(14)
    arrived(2)
    start(10)
    for number in (3, 8, 9, 11, 12, 13, 14, 10):
        arrived(number)

    loads[3].wait()
    chunk_pairs = pairs // CHUNKS

    def near_copy(chunk, j):
        rows = pl.ds(chunk * chunk_pairs, chunk_pairs)
        return pltpu.make_async_remote_copy(
            src_ref=near_send.at[j, rows],
            dst_ref=near_recv.at[j, rows],
            send_sem=near_ssem.at[chunk, j],
            recv_sem=near_rsem.at[chunk, j],
            device_id=(me_l, peers[j]),
            device_id_type=MESH,
        )

    def near_leaf(t):
        total = None
        for k in range(NEAR):
            left_side = wide[:, W + t + near_offset[t, k]].reshape(RHS * cols, LEAF)
            term = dot_nt(left_side, blocks[:, t, k].reshape(OPS * rank, LEAF))
            total = term if total is None else total + term
        return total

    for chunk in range(CHUNKS):

        @pl.loop(0, chunk_pairs)
        def _(step):
            pair = chunk * chunk_pairs + step
            first = near_leaf(2 * pair)
            second = near_leaf(2 * pair + 1)
            packed = jnp.concatenate(
                [
                    first[:, : 2 * rank],
                    second[:, : 2 * rank],
                    first[:, 2 * rank :],
                    second[:, 2 * rank :],
                ],
                axis=-1,
            ).astype(BF16)
            near_recv[0, pair] = packed[:cols]
            for j in range(1, RHS):
                near_send[j, pair] = packed[j * cols : (j + 1) * cols]

        for j in (2, 3, 1):
            near_copy(chunk, j).start()

    for step in range(1, groups):
        root_copy(step).wait_recv()
    for i in (4, 5, 6):
        loads[i].wait()

    def top_row(height):
        return groups - groups // 2 ** (height - 1)

    def top_base(height):
        return sum(groups // 2**h + 6 for h in range(1, height))

    def top_coef(height, index):
        if height == 0:
            return roots[3 + index]
        return upper_coef[top_base(height) + 3 + index]

    for height in range(1, TOPL):
        for q in range(groups // 2**height):
            pair = joined(top_coef(height - 1, 2 * q), top_coef(height - 1, 2 * q + 1))
            upper_coef[top_base(height) + 3 + q] = twice(dot_nt(pair, top[top_row(height) + q]))

    def top_field(height):
        cluster = me_l // 2**height
        odd = cluster % 2
        near_by = [
            top_coef(height, cluster + s) for s in (-2 - odd, 2 - 4 * odd, 3 - odd)
        ]
        sources = jnp.concatenate([joined(near_by[0], near_by[1]), near_by[2][:, :rank]], axis=-1)
        terms = []
        for o in range(OPS):
            matrix = root_k[o, 0] if height == 0 else upper_k[o, top_row(height) + cluster]
            terms.append(dot_nt(sources, matrix))
        return jnp.concatenate(terms, axis=0)

    running = top_field(TOPL - 1)
    for height in range(TOPL - 1, 0, -1):
        pushed = dot_nn(running.astype(BF16), top[top_row(height) + me_l // 2**height])
        child = (me_l // 2 ** (height - 1)) % 2
        half = jnp.where(child == 0, pushed[:, :rank], pushed[:, rank:])
        running = top_field(height - 1) + half

    fields[1] = running
    for height in reversed(range(depth)):
        count = leaves >> height + 1
        offset = leaves - 2 * count
        for p in range(count):
            pushed = dot_nn(fields[count + p].astype(BF16), local[0, offset + p])
            fields[2 * (count + p)] = pushed[:, :rank]
            fields[2 * (count + p) + 1] = pushed[:, rank:]

    for j in range(1, RHS):
        near_copy(0, j).wait_recv()
    slots = (me_r, side, across, diagonal)
    for chunk in range(CHUNKS):
        if chunk:
            for j in range(1, RHS):
                near_copy(chunk, j).wait_recv()

        for step in range(chunk_pairs):
            pair = chunk * chunk_pairs + step
            near = [near_recv[slots[r], pair].astype(F32) for r in range(RHS)]
            for e in range(2):
                t = 2 * pair + e
                leaf_field = (fields[leaves + t] + coupled[t]).astype(BF16)
                far = dot_nn(leaf_field, basis[t])
                for o in range(OPS):
                    at = (2 * e + o if o < 2 else 4 + e) * rank
                    row = jnp.concatenate([piece[:, at : at + rank] for piece in near], axis=-1)
                    out[o, :, t * LEAF : (t + 1) * LEAF] = (
                        far[o * cols : (o + 1) * cols] + row
                    ).astype(BF16)

    for number in copies:
        run(number, "wait_send")
    for step in range(1, groups):
        root_copy(step).wait_send()
    for chunk in range(CHUNKS):
        for j in range(1, RHS):
            near_copy(chunk, j).wait_send()


def per_device(
    points,
    leaf_basis,
    local_transfer,
    top_transfer,
    leaf_coupling,
    root_coupling,
    upper_coupling,
    near_blocks,
    near_offset,
    far_offset,
):
    groups = lax.axis_size("leaf")
    cols, count = points.shape
    leaves, rank, _ = leaf_basis.shape
    upper_rows = sum(groups // 2**h + 6 for h in range(1, TOPL))
    anywhere = pl.BlockSpec(memory_space=pl.ANY)
    near_shape = (RHS, leaves // 2, cols, 2 * OPS * rank)
    return pl.pallas_call(
        functools.partial(kernel, groups),
        out_shape=jax.ShapeDtypeStruct((OPS, cols, count), BF16),
        in_specs=[
            pl.BlockSpec(memory_space=pltpu.VMEM),
            pl.BlockSpec(memory_space=pltpu.SMEM),
            pl.BlockSpec(memory_space=pltpu.SMEM),
        ]
        + [anywhere] * 7,
        out_specs=pl.BlockSpec(memory_space=pltpu.VMEM),
        scratch_shapes=[
            pltpu.VMEM(leaf_basis.shape, BF16),
            pltpu.VMEM(local_transfer.shape, BF16),
            pltpu.VMEM(top_transfer.shape, BF16),
            pltpu.VMEM(leaf_coupling.shape, BF16),
            pltpu.VMEM(root_coupling.shape, BF16),
            pltpu.VMEM(upper_coupling.shape, BF16),
            pltpu.VMEM(near_blocks.shape, BF16),
            pltpu.VMEM((RHS, leaves + 2 * W, cols, LEAF), BF16),
            pltpu.VMEM((leaves + 2 * W, cols, 2 * rank), BF16),
            pltpu.VMEM((leaves - 1, cols, 2 * rank), BF16),
            pltpu.VMEM((groups + 6, cols, 2 * rank), BF16),
            pltpu.VMEM((upper_rows, cols, 2 * rank), BF16),
            pltpu.VMEM((leaves, OPS * cols, rank), F32),
            pltpu.VMEM((2 * leaves, OPS * cols, rank), F32),
            pltpu.VMEM(near_shape, BF16),
            pltpu.VMEM(near_shape, BF16),
            pltpu.SemaphoreType.DMA((7,)),
            pltpu.SemaphoreType.DMA((17,)),
            pltpu.SemaphoreType.DMA((17,)),
            pltpu.SemaphoreType.DMA((groups - 1,)),
            pltpu.SemaphoreType.DMA((groups - 1,)),
            pltpu.SemaphoreType.DMA((CHUNKS, RHS)),
            pltpu.SemaphoreType.DMA((CHUNKS, RHS)),
        ],
        compiler_params=pltpu.CompilerParams(
            collective_id=0, has_side_effects=True, vmem_limit_bytes=56 * 1024 * 1024
        ),
        cost_estimate=pl.CostEstimate(
            flops=900_000_000, bytes_accessed=17_000_000, transcendentals=0
        ),
    )(
        points,
        near_offset,
        far_offset,
        leaf_basis,
        local_transfer,
        top_transfer,
        leaf_coupling,
        root_coupling,
        upper_coupling,
        near_blocks,
    )


def solution(mesh):
    placed = (
        P("rhs", "leaf"),
        P("leaf", None, None),
        P("leaf", None, None, None),
        P(),
        P(None, "leaf", None, None),
        P(None, "leaf", None, None),
        P(),
        P(None, "leaf", None, "rhs", None),
        P("leaf", None),
        P("leaf", None),
    )
    return jax.shard_map(
        per_device, mesh=mesh, in_specs=placed, out_specs=P(None, "rhs", "leaf"), check_vma=False
    )
```

```python
import functools

import jax
import jax.numpy as jnp
from jax import lax
from jax.experimental import pallas as pl
from jax.experimental.pallas import tpu as pltpu
from jax.sharding import PartitionSpec as P

LEAF = 256
OPS = 3
W = 8
NEAR = 3
FAR = 5
TOPL = 3
RHS = 4
CHUNKS = 4
UNROLL = 8
MESH = pl.DeviceIdType.MESH
F32 = jnp.float32
BF16 = jnp.bfloat16


def dot_nt(a, b):
    return lax.dot_general(a, b, (((1,), (1,)), ((), ())), preferred_element_type=F32)


def dot_nn(a, b):
    return lax.dot_general(a, b, (((1,), (0,)), ((), ())), preferred_element_type=F32)


def twice(values):
    return jnp.concatenate([values, values], axis=-1).astype(BF16)


def kernel(
    groups,
    points_hbm,
    near_hbm,
    far_hbm,
    basis_hbm,
    local_hbm,
    top_hbm,
    coupling_hbm,
    root_hbm,
    upper_hbm,
    blocks_hbm,
    out_hbm,
    points,
    near_offset,
    far_offset,
    out,
    basis,
    local,
    top,
    coupling,
    root_k,
    upper_k,
    blocks,
    wide,
    coef,
    level_coef,
    roots,
    upper_coef,
    coupled,
    fields,
    far_part,
    near_send,
    near_recv,
    in_sem,
    send_sem,
    recv_sem,
    root_send,
    root_recv,
    near_ssem,
    near_rsem,
    out_sem,
):
    cols = points.shape[0]
    leaves = basis.shape[0]
    rank = basis.shape[1]
    pairs = leaves // 2
    me_l = lax.axis_index("leaf")
    me_r = lax.axis_index("rhs")
    side = me_r + 1 - 2 * (me_r % 2)
    across = (me_r + 2) % 4
    diagonal = (side + 2) % 4
    peers = (me_r, side, across, diagonal)
    has_left = me_l > 0
    has_right = me_l < groups - 1
    top_w = W + leaves

    barrier = pltpu.get_barrier_semaphore()
    for peer in peers[1:]:
        pl.semaphore_signal(barrier, inc=1, device_id=(me_l, peer), device_id_type=MESH)
    for step in range(1, groups):
        pl.semaphore_signal(
            barrier, inc=1, device_id=((me_l + step) % groups, me_r), device_id_type=MESH
        )

    loads = [
        pltpu.make_async_copy(source, target, in_sem.at[i])
        for i, (source, target) in enumerate(
            [
                (points_hbm, points),
                (basis_hbm, basis),
                (local_hbm, local),
                (far_hbm, far_offset),
                (near_hbm, near_offset),
                (coupling_hbm, coupling),
                (blocks_hbm, blocks),
                (top_hbm, top),
                (root_hbm, root_k),
                (upper_hbm, upper_k),
            ]
        )
    ]
    for load in loads:
        load.start()

    low, high = pl.ds(0, W), pl.ds(top_w, W)
    head, tail = pl.ds(W, W), pl.ds(leaves, W)
    middle = pl.ds(2 * W, leaves - 2 * W)
    body = pl.ds(W, leaves)

    @pl.when(jnp.logical_not(has_left))
    def _():
        wide[:, 0:W] = jnp.zeros((RHS, W, cols, LEAF), BF16)
        coef[0:W] = jnp.zeros((W, cols, 2 * rank), BF16)

    @pl.when(jnp.logical_not(has_right))
    def _():
        wide[:, top_w : top_w + W] = jnp.zeros((RHS, W, cols, LEAF), BF16)
        coef[top_w : top_w + W] = jnp.zeros((W, cols, 2 * rank), BF16)

    roots[0:3] = jnp.zeros((3, cols, 2 * rank), BF16)
    roots[3 + groups : 6 + groups] = jnp.zeros((3, cols, 2 * rank), BF16)
    upper_coef[...] = jnp.zeros(upper_coef.shape, BF16)

    loads[0].wait()
    for t in range(leaves):
        wide[0, W + t] = points[:, t * LEAF : (t + 1) * LEAF]

    right = (me_l + 1) % groups
    left = (me_l + groups - 1) % groups

    def remote(number, source, target, leaf, rhs):
        return pltpu.make_async_remote_copy(
            src_ref=source,
            dst_ref=target,
            send_sem=send_sem.at[number],
            recv_sem=recv_sem.at[number],
            device_id=(leaf, rhs),
            device_id_type=MESH,
        )

    def part(slot, where):
        return wide.at[slot, where]

    copies = {
        0: (part(0, head), part(2, head), me_l, across),
        1: (part(0, tail), part(2, tail), me_l, across),
        2: (part(0, middle), part(2, middle), me_l, across),
        3: (part(0, body), part(1, body), me_l, side),
        4: (part(0, tail), part(0, low), right, me_r),
        5: (part(0, head), part(0, high), left, me_r),
        6: (part(2, tail), part(2, low), right, me_r),
        7: (part(2, head), part(2, high), left, me_r),
        8: (part(2, head), part(3, head), me_l, side),
        9: (part(2, tail), part(3, tail), me_l, side),
        10: (part(2, middle), part(3, middle), me_l, side),
        11: (part(0, low), part(1, low), me_l, side),
        12: (part(0, high), part(1, high), me_l, side),
        13: (part(2, low), part(3, low), me_l, side),
        14: (part(2, high), part(3, high), me_l, side),
        15: (coef.at[tail], coef.at[low], right, me_r),
        16: (coef.at[head], coef.at[high], left, me_r),
    }
    to_right = (4, 6, 15)
    to_left = (5, 7, 16)
    from_low = (11, 13)
    from_high = (12, 14)

    def guard(number, receiving):
        if number in to_right:
            return has_left if receiving else has_right
        if number in to_left:
            return has_right if receiving else has_left
        if number in from_low:
            return has_left
        if number in from_high:
            return has_right
        return None

    def run(number, action):
        condition = guard(number, action == "wait_recv")

        def go():
            getattr(remote(number, *copies[number]), action)()

        if condition is None:
            go()
        else:
            pl.when(condition)(go)

    def start(number):
        run(number, "start")

    def arrived(number):
        run(number, "wait_recv")

    pl.semaphore_wait(barrier, len(peers) - 1 + groups - 1)
    for number in (0, 1, 4, 5, 2, 3):
        start(number)

    first_half = lax.broadcasted_iota(jnp.int32, (cols, 2 * rank), 1) < rank

    def joined(a, b):
        return jnp.where(first_half, a.astype(F32), b.astype(F32)).astype(BF16)

    loads[1].wait()

    @pl.loop(0, leaves // UNROLL)
    def _(step):
        for u in range(UNROLL):
            t = step * UNROLL + u
            coef[W + t] = twice(dot_nt(wide[0, W + t], basis[t]))

    start(15)
    start(16)

    arrived(0)
    start(7)
    start(8)
    arrived(1)
    start(6)
    start(9)

    loads[2].wait()
    depth = leaves.bit_length() - 1
    offset = 0
    base = 0
    for height in range(depth):
        count = leaves >> height + 1
        for p in range(count):
            if height == 0:
                pair = joined(coef[W + 2 * p], coef[W + 2 * p + 1])
            else:
                pair = joined(level_coef[base + 2 * p], level_coef[base + 2 * p + 1])
            level_coef[offset + p] = twice(dot_nt(pair, local[0, offset + p]))
        base = offset
        offset += count
    roots[3 + me_l] = level_coef[leaves - 2]

    def root_copy(step):
        return pltpu.make_async_remote_copy(
            src_ref=roots.at[3 + me_l],
            dst_ref=roots.at[3 + me_l],
            send_sem=root_send.at[step - 1],
            recv_sem=root_recv.at[step - 1],
            device_id=((me_l + step) % groups, me_r),
            device_id_type=MESH,
        )

    for step in range(1, groups):
        root_copy(step).start()

    arrived(4)
    start(11)
    arrived(5)
    start(12)
    arrived(2)
    start(10)
    arrived(15)
    arrived(16)

    for i in (3, 4, 5):
        loads[i].wait()

    def couple_leaves(begin, end):
        @pl.loop(begin, end)
        def _(step):
            for u in range(UNROLL):
                t = step * UNROLL + u
                picked = [coef[W + t + far_offset[k, t]] for k in range(FAR)]
                pieces = [joined(picked[k], picked[k + 1]) for k in range(0, FAR - 1, 2)]
                pieces.append(picked[FAR - 1][:, :rank])
                sources = jnp.concatenate(pieces, axis=-1)
                matrix = coupling[:, t].reshape(OPS * rank, FAR * rank)
                product = dot_nt(sources, matrix)
                for o in range(OPS):
                    coupled[t, o * cols : (o + 1) * cols] = product[:, o * rank : (o + 1) * rank]

    steps = leaves // UNROLL
    couple_leaves(0, steps // 2)
    arrived(6)
    start(13)
    arrived(7)
    start(14)
    couple_leaves(steps // 2, steps)
    for number in (3, 8, 9, 11, 12, 10, 13, 14):
        arrived(number)

    loads[6].wait()
    chunk_pairs = pairs // CHUNKS

    def near_copy(chunk, j):
        rows = pl.ds(chunk * chunk_pairs, chunk_pairs)
        return pltpu.make_async_remote_copy(
            src_ref=near_send.at[j, rows],
            dst_ref=near_recv.at[j, rows],
            send_sem=near_ssem.at[chunk, j],
            recv_sem=near_rsem.at[chunk, j],
            device_id=(me_l, peers[j]),
            device_id_type=MESH,
        )

    def near_leaf(t):
        total = None
        for k in range(NEAR):
            left_side = wide[:, W + t + near_offset[k, t]].reshape(RHS * cols, LEAF)
            term = dot_nt(left_side, blocks[:, t, k].reshape(OPS * rank, LEAF))
            total = term if total is None else total + term
        return total

    @pl.loop(0, CHUNKS)
    def _(chunk):
        for step in range(chunk_pairs):
            pair = chunk * chunk_pairs + step
            first = near_leaf(2 * pair)
            second = near_leaf(2 * pair + 1)
            packed = jnp.concatenate(
                [
                    first[:, : 2 * rank],
                    second[:, : 2 * rank],
                    first[:, 2 * rank :],
                    second[:, 2 * rank :],
                ],
                axis=-1,
            ).astype(BF16)
            near_recv[0, pair] = packed[:cols]
            for j in range(1, RHS):
                near_send[j, pair] = packed[j * cols : (j + 1) * cols]

        for j in (2, 3, 1):
            near_copy(chunk, j).start()

    for step in range(1, groups):
        root_copy(step).wait_recv()
    for i in (7, 8, 9):
        loads[i].wait()

    def top_row(height):
        return groups - groups // 2 ** (height - 1)

    def top_base(height):
        return sum(groups // 2**h + 6 for h in range(1, height))

    def top_coef(height, index):
        if height == 0:
            return roots[3 + index]
        return upper_coef[top_base(height) + 3 + index]

    for height in range(1, TOPL):
        for q in range(groups // 2**height):
            pair = joined(top_coef(height - 1, 2 * q), top_coef(height - 1, 2 * q + 1))
            upper_coef[top_base(height) + 3 + q] = twice(dot_nt(pair, top[top_row(height) + q]))

    def top_field(height):
        cluster = me_l // 2**height
        odd = cluster % 2
        near_by = [
            top_coef(height, cluster + s) for s in (-2 - odd, 2 - 4 * odd, 3 - odd)
        ]
        sources = jnp.concatenate([joined(near_by[0], near_by[1]), near_by[2][:, :rank]], axis=-1)
        terms = []
        for o in range(OPS):
            matrix = root_k[o, 0] if height == 0 else upper_k[o, top_row(height) + cluster]
            terms.append(dot_nt(sources, matrix))
        return jnp.concatenate(terms, axis=0)

    running = top_field(TOPL - 1)
    for height in range(TOPL - 1, 0, -1):
        pushed = dot_nn(running.astype(BF16), top[top_row(height) + me_l // 2**height])
        child = (me_l // 2 ** (height - 1)) % 2
        half = jnp.where(child == 0, pushed[:, :rank], pushed[:, rank:])
        running = top_field(height - 1) + half

    fields[1] = running
    for height in reversed(range(depth)):
        count = leaves >> height + 1
        offset = leaves - 2 * count
        for p in range(count):
            pushed = dot_nn(fields[count + p].astype(BF16), local[0, offset + p])
            fields[2 * (count + p)] = pushed[:, :rank]
            fields[2 * (count + p) + 1] = pushed[:, rank:]

    for t in range(leaves):
        leaf_field = (fields[leaves + t] + coupled[t]).astype(BF16)
        far_part[t] = dot_nn(leaf_field, basis[t])

    slots = (me_r, side, across, diagonal)
    chunk_points = 2 * chunk_pairs * LEAF

    def out_copy(chunk):
        where = pl.ds(pl.multiple_of(chunk * chunk_points, chunk_points), chunk_points)
        return pltpu.make_async_copy(
            out.at[chunk], out_hbm.at[:, :, where], out_sem.at[chunk]
        )

    @pl.loop(0, CHUNKS)
    def _(chunk):
        for j in range(1, RHS):
            near_copy(chunk, j).wait_recv()
        for step in range(chunk_pairs):
            pair = chunk * chunk_pairs + step
            near = [near_recv[slots[r], pair].astype(F32) for r in range(RHS)]
            for e in range(2):
                place = 2 * step + e
                far = far_part[2 * pair + e]
                for o in range(OPS):
                    at = (2 * e + o if o < 2 else 4 + e) * rank
                    row = jnp.concatenate([piece[:, at : at + rank] for piece in near], axis=-1)
                    out[chunk, o, :, place * LEAF : (place + 1) * LEAF] = (
                        far[o * cols : (o + 1) * cols] + row
                    ).astype(BF16)
        out_copy(chunk).start()

    for chunk in range(CHUNKS):
        out_copy(chunk).wait()
    for number in copies:
        run(number, "wait_send")
    for step in range(1, groups):
        root_copy(step).wait_send()
    for chunk in range(CHUNKS):
        for j in range(1, RHS):
            near_copy(chunk, j).wait_send()


def per_device(
    points,
    leaf_basis,
    local_transfer,
    top_transfer,
    leaf_coupling,
    root_coupling,
    upper_coupling,
    near_blocks,
    near_offset,
    far_offset,
):
    groups = lax.axis_size("leaf")
    cols, count = points.shape
    leaves, rank, _ = leaf_basis.shape
    upper_rows = sum(groups // 2**h + 6 for h in range(1, TOPL))
    anywhere = pl.BlockSpec(memory_space=pl.ANY)
    near_shape = (RHS, leaves // 2, cols, 2 * OPS * rank)
    return pl.pallas_call(
        functools.partial(kernel, groups),
        out_shape=jax.ShapeDtypeStruct((OPS, cols, count), BF16),
        in_specs=[anywhere] * 10,
        out_specs=anywhere,
        scratch_shapes=[
            pltpu.VMEM(points.shape, BF16),
            pltpu.SMEM((NEAR, leaves), jnp.int32),
            pltpu.SMEM((FAR, leaves), jnp.int32),
            pltpu.VMEM((CHUNKS, OPS, cols, count // CHUNKS), BF16),
            pltpu.VMEM(leaf_basis.shape, BF16),
            pltpu.VMEM(local_transfer.shape, BF16),
            pltpu.VMEM(top_transfer.shape, BF16),
            pltpu.VMEM(leaf_coupling.shape, BF16),
            pltpu.VMEM(root_coupling.shape, BF16),
            pltpu.VMEM(upper_coupling.shape, BF16),
            pltpu.VMEM(near_blocks.shape, BF16),
            pltpu.VMEM((RHS, leaves + 2 * W, cols, LEAF), BF16),
            pltpu.VMEM((leaves + 2 * W, cols, 2 * rank), BF16),
            pltpu.VMEM((leaves - 1, cols, 2 * rank), BF16),
            pltpu.VMEM((groups + 6, cols, 2 * rank), BF16),
            pltpu.VMEM((upper_rows, cols, 2 * rank), BF16),
            pltpu.VMEM((leaves, OPS * cols, rank), F32),
            pltpu.VMEM((2 * leaves, OPS * cols, rank), F32),
            pltpu.VMEM((leaves, OPS * cols, LEAF), F32),
            pltpu.VMEM(near_shape, BF16),
            pltpu.VMEM(near_shape, BF16),
            pltpu.SemaphoreType.DMA((10,)),
            pltpu.SemaphoreType.DMA((17,)),
            pltpu.SemaphoreType.DMA((17,)),
            pltpu.SemaphoreType.DMA((groups - 1,)),
            pltpu.SemaphoreType.DMA((groups - 1,)),
            pltpu.SemaphoreType.DMA((CHUNKS, RHS)),
            pltpu.SemaphoreType.DMA((CHUNKS, RHS)),
            pltpu.SemaphoreType.DMA((CHUNKS,)),
        ],
        compiler_params=pltpu.CompilerParams(
            collective_id=0, has_side_effects=True, vmem_limit_bytes=56 * 1024 * 1024
        ),
        cost_estimate=pl.CostEstimate(
            flops=900_000_000, bytes_accessed=17_000_000, transcendentals=0
        ),
    )(
        points,
        near_offset.T,
        far_offset.T,
        leaf_basis,
        local_transfer,
        top_transfer,
        leaf_coupling,
        root_coupling,
        upper_coupling,
        near_blocks,
    )


def solution(mesh):
    placed = (
        P("rhs", "leaf"),
        P("leaf", None, None),
        P("leaf", None, None, None),
        P(),
        P(None, "leaf", None, None),
        P(None, "leaf", None, None),
        P(),
        P(None, "leaf", None, "rhs", None),
        P("leaf", None),
        P("leaf", None),
    )
    return jax.shard_map(
        per_device, mesh=mesh, in_specs=placed, out_specs=P(None, "rhs", "leaf"), check_vma=False
    )
```

```python
import functools

import jax
import jax.numpy as jnp
from jax import lax
from jax.experimental import pallas as pl
from jax.experimental.pallas import tpu as pltpu
from jax.sharding import PartitionSpec as P

LEAF = 256
OPS = 3
W = 8
NEAR = 3
FAR = 5
TOPL = 3
RHS = 4
CHUNKS = 8
PARTS = 2
UNROLL = 8
MESH = pl.DeviceIdType.MESH
F32 = jnp.float32
BF16 = jnp.bfloat16


def dot_nt(a, b):
    return lax.dot_general(a, b, (((1,), (1,)), ((), ())), preferred_element_type=F32)


def dot_nn(a, b):
    return lax.dot_general(a, b, (((1,), (0,)), ((), ())), preferred_element_type=F32)


def twice(values):
    return jnp.concatenate([values, values], axis=-1).astype(BF16)


def kernel(
    groups,
    points_hbm,
    near_hbm,
    far_hbm,
    basis_hbm,
    local_hbm,
    top_hbm,
    coupling_hbm,
    root_hbm,
    upper_hbm,
    blocks_hbm,
    out_hbm,
    points,
    near_offset,
    far_offset,
    out,
    basis,
    local,
    top,
    coupling,
    root_k,
    upper_k,
    blocks,
    wide,
    coef,
    level_coef,
    roots,
    upper_coef,
    coupled,
    fields,
    far_part,
    near_send,
    near_recv,
    in_sem,
    send_sem,
    recv_sem,
    root_send,
    root_recv,
    near_ssem,
    near_rsem,
    out_sem,
):
    cols = points.shape[0]
    leaves = basis.shape[0]
    rank = basis.shape[1]
    pairs = leaves // 2
    me_l = lax.axis_index("leaf")
    me_r = lax.axis_index("rhs")
    side = me_r + 1 - 2 * (me_r % 2)
    across = (me_r + 2) % 4
    diagonal = (side + 2) % 4
    peers = (me_r, side, across, diagonal)
    has_left = me_l > 0
    has_right = me_l < groups - 1
    top_w = W + leaves

    barrier = pltpu.get_barrier_semaphore()
    for peer in peers[1:]:
        pl.semaphore_signal(barrier, inc=1, device_id=(me_l, peer), device_id_type=MESH)
    for step in range(1, groups):
        pl.semaphore_signal(
            barrier, inc=1, device_id=((me_l + step) % groups, me_r), device_id_type=MESH
        )

    loads = [
        pltpu.make_async_copy(source, target, in_sem.at[i])
        for i, (source, target) in enumerate(
            [
                (points_hbm, points),
                (basis_hbm, basis),
                (local_hbm, local),
                (far_hbm, far_offset),
                (near_hbm, near_offset),
                (coupling_hbm, coupling),
                (blocks_hbm, blocks),
                (top_hbm, top),
                (root_hbm, root_k),
                (upper_hbm, upper_k),
            ]
        )
    ]
    for load in loads:
        load.start()

    low, high = pl.ds(0, W), pl.ds(top_w, W)
    head, tail = pl.ds(W, W), pl.ds(leaves, W)
    middle = pl.ds(2 * W, leaves - 2 * W)
    body = pl.ds(W, leaves)

    @pl.when(jnp.logical_not(has_left))
    def _():
        wide[:, 0:W] = jnp.zeros((RHS, W, cols, LEAF), BF16)
        coef[0:W] = jnp.zeros((W, cols, 2 * rank), BF16)

    @pl.when(jnp.logical_not(has_right))
    def _():
        wide[:, top_w : top_w + W] = jnp.zeros((RHS, W, cols, LEAF), BF16)
        coef[top_w : top_w + W] = jnp.zeros((W, cols, 2 * rank), BF16)

    roots[0:3] = jnp.zeros((3, cols, 2 * rank), BF16)
    roots[3 + groups : 6 + groups] = jnp.zeros((3, cols, 2 * rank), BF16)
    upper_coef[...] = jnp.zeros(upper_coef.shape, BF16)

    loads[0].wait()
    for t in range(leaves):
        wide[0, W + t] = points[:, t * LEAF : (t + 1) * LEAF]

    right = (me_l + 1) % groups
    left = (me_l + groups - 1) % groups

    def remote(number, source, target, leaf, rhs):
        return pltpu.make_async_remote_copy(
            src_ref=source,
            dst_ref=target,
            send_sem=send_sem.at[number],
            recv_sem=recv_sem.at[number],
            device_id=(leaf, rhs),
            device_id_type=MESH,
        )

    def part(slot, where):
        return wide.at[slot, where]

    copies = {
        0: (part(0, head), part(2, head), me_l, across),
        1: (part(0, tail), part(2, tail), me_l, across),
        2: (part(0, middle), part(2, middle), me_l, across),
        3: (part(0, body), part(1, body), me_l, side),
        4: (part(0, tail), part(0, low), right, me_r),
        5: (part(0, head), part(0, high), left, me_r),
        6: (part(2, tail), part(2, low), right, me_r),
        7: (part(2, head), part(2, high), left, me_r),
        8: (part(2, head), part(3, head), me_l, side),
        9: (part(2, tail), part(3, tail), me_l, side),
        10: (part(2, middle), part(3, middle), me_l, side),
        11: (part(0, low), part(1, low), me_l, side),
        12: (part(0, high), part(1, high), me_l, side),
        13: (part(2, low), part(3, low), me_l, side),
        14: (part(2, high), part(3, high), me_l, side),
        15: (coef.at[tail], coef.at[low], right, me_r),
        16: (coef.at[head], coef.at[high], left, me_r),
    }
    to_right = (4, 6, 15)
    to_left = (5, 7, 16)
    from_low = (11, 13)
    from_high = (12, 14)

    def guard(number, receiving):
        if number in to_right:
            return has_left if receiving else has_right
        if number in to_left:
            return has_right if receiving else has_left
        if number in from_low:
            return has_left
        if number in from_high:
            return has_right
        return None

    def run(number, action):
        condition = guard(number, action == "wait_recv")

        def go():
            getattr(remote(number, *copies[number]), action)()

        if condition is None:
            go()
        else:
            pl.when(condition)(go)

    def start(number):
        run(number, "start")

    def arrived(number):
        run(number, "wait_recv")

    pl.semaphore_wait(barrier, len(peers) - 1 + groups - 1)
    for number in (0, 1, 4, 5, 2, 3):
        start(number)

    first_half = lax.broadcasted_iota(jnp.int32, (cols, 2 * rank), 1) < rank

    def joined(a, b):
        return jnp.where(first_half, a.astype(F32), b.astype(F32)).astype(BF16)

    loads[1].wait()

    @pl.loop(0, leaves // UNROLL)
    def _(step):
        for u in range(UNROLL):
            t = step * UNROLL + u
            coef[W + t] = twice(dot_nt(wide[0, W + t], basis[t]))

    start(15)
    start(16)

    arrived(0)
    start(7)
    start(8)
    arrived(1)
    start(6)
    start(9)

    loads[2].wait()
    depth = leaves.bit_length() - 1
    offset = 0
    base = 0
    for height in range(depth):
        count = leaves >> height + 1
        for p in range(count):
            if height == 0:
                pair = joined(coef[W + 2 * p], coef[W + 2 * p + 1])
            else:
                pair = joined(level_coef[base + 2 * p], level_coef[base + 2 * p + 1])
            level_coef[offset + p] = twice(dot_nt(pair, local[0, offset + p]))
        base = offset
        offset += count
    roots[3 + me_l] = level_coef[leaves - 2]

    def root_copy(step):
        return pltpu.make_async_remote_copy(
            src_ref=roots.at[3 + me_l],
            dst_ref=roots.at[3 + me_l],
            send_sem=root_send.at[step - 1],
            recv_sem=root_recv.at[step - 1],
            device_id=((me_l + step) % groups, me_r),
            device_id_type=MESH,
        )

    for step in range(1, groups):
        root_copy(step).start()

    arrived(4)
    start(11)
    arrived(5)
    start(12)
    arrived(2)
    start(10)
    arrived(15)
    arrived(16)

    for i in (3, 4, 5):
        loads[i].wait()

    def couple_leaves(begin, end):
        @pl.loop(begin, end)
        def _(step):
            for u in range(UNROLL):
                t = step * UNROLL + u
                picked = [coef[W + t + far_offset[k, t]] for k in range(FAR)]
                pieces = [joined(picked[k], picked[k + 1]) for k in range(0, FAR - 1, 2)]
                pieces.append(picked[FAR - 1][:, :rank])
                sources = jnp.concatenate(pieces, axis=-1)
                matrix = coupling[:, t].reshape(OPS * rank, FAR * rank)
                product = dot_nt(sources, matrix)
                for o in range(OPS):
                    coupled[t, o * cols : (o + 1) * cols] = product[:, o * rank : (o + 1) * rank]

    steps = leaves // UNROLL
    couple_leaves(0, steps // 2)
    arrived(6)
    start(13)
    arrived(7)
    start(14)
    couple_leaves(steps // 2, steps)
    for number in (3, 8, 9, 11, 12, 10, 13, 14):
        arrived(number)

    loads[6].wait()
    chunk_pairs = pairs // CHUNKS

    def near_copy(chunk, j):
        rows = pl.ds(chunk * chunk_pairs, chunk_pairs)
        return pltpu.make_async_remote_copy(
            src_ref=near_send.at[j, rows],
            dst_ref=near_recv.at[j, rows],
            send_sem=near_ssem.at[chunk, j],
            recv_sem=near_rsem.at[chunk, j],
            device_id=(me_l, peers[j]),
            device_id_type=MESH,
        )

    def near_leaf(t):
        total = None
        for k in range(NEAR):
            left_side = wide[:, W + t + near_offset[k, t]].reshape(RHS * cols, LEAF)
            term = dot_nt(left_side, blocks[:, t, k].reshape(OPS * rank, LEAF))
            total = term if total is None else total + term
        return total

    @pl.loop(0, CHUNKS)
    def _(chunk):
        for step in range(chunk_pairs):
            pair = chunk * chunk_pairs + step
            first = near_leaf(2 * pair)
            second = near_leaf(2 * pair + 1)
            packed = jnp.concatenate(
                [
                    first[:, : 2 * rank],
                    second[:, : 2 * rank],
                    first[:, 2 * rank :],
                    second[:, 2 * rank :],
                ],
                axis=-1,
            ).astype(BF16)
            near_recv[0, pair] = packed[:cols]
            for j in range(1, RHS):
                near_send[j, pair] = packed[j * cols : (j + 1) * cols]

        for j in (2, 3, 1):
            near_copy(chunk, j).start()

    for step in range(1, groups):
        root_copy(step).wait_recv()
    for i in (7, 8, 9):
        loads[i].wait()

    def top_row(height):
        return groups - groups // 2 ** (height - 1)

    def top_base(height):
        return sum(groups // 2**h + 6 for h in range(1, height))

    def top_coef(height, index):
        if height == 0:
            return roots[3 + index]
        return upper_coef[top_base(height) + 3 + index]

    for height in range(1, TOPL):
        for q in range(groups // 2**height):
            pair = joined(top_coef(height - 1, 2 * q), top_coef(height - 1, 2 * q + 1))
            upper_coef[top_base(height) + 3 + q] = twice(dot_nt(pair, top[top_row(height) + q]))

    def top_field(height):
        cluster = me_l // 2**height
        odd = cluster % 2
        near_by = [
            top_coef(height, cluster + s) for s in (-2 - odd, 2 - 4 * odd, 3 - odd)
        ]
        sources = jnp.concatenate([joined(near_by[0], near_by[1]), near_by[2][:, :rank]], axis=-1)
        terms = []
        for o in range(OPS):
            matrix = root_k[o, 0] if height == 0 else upper_k[o, top_row(height) + cluster]
            terms.append(dot_nt(sources, matrix))
        return jnp.concatenate(terms, axis=0)

    running = top_field(TOPL - 1)
    for height in range(TOPL - 1, 0, -1):
        pushed = dot_nn(running.astype(BF16), top[top_row(height) + me_l // 2**height])
        child = (me_l // 2 ** (height - 1)) % 2
        half = jnp.where(child == 0, pushed[:, :rank], pushed[:, rank:])
        running = top_field(height - 1) + half

    fields[1] = running
    for height in reversed(range(depth)):
        count = leaves >> height + 1
        offset = leaves - 2 * count
        for p in range(count):
            pushed = dot_nn(fields[count + p].astype(BF16), local[0, offset + p])
            fields[2 * (count + p)] = pushed[:, :rank]
            fields[2 * (count + p) + 1] = pushed[:, rank:]

    for t in range(leaves):
        leaf_field = (fields[leaves + t] + coupled[t]).astype(BF16)
        far_part[t] = dot_nn(leaf_field, basis[t])

    slots = (me_r, side, across, diagonal)
    chunk_points = 2 * chunk_pairs * LEAF

    def out_copy(chunk):
        where = pl.ds(pl.multiple_of(chunk * chunk_points, chunk_points), chunk_points)
        return pltpu.make_async_copy(
            out.at[chunk], out_hbm.at[:, :, where], out_sem.at[chunk]
        )

    @pl.loop(0, CHUNKS)
    def _(chunk):
        for j in range(1, RHS):
            near_copy(chunk, j).wait_recv()
        for step in range(chunk_pairs):
            pair = chunk * chunk_pairs + step
            near = [near_recv[slots[r], pair].astype(F32) for r in range(RHS)]
            for e in range(2):
                place = 2 * step + e
                far = far_part[2 * pair + e]
                for o in range(OPS):
                    at = (2 * e + o if o < 2 else 4 + e) * rank
                    row = jnp.concatenate([piece[:, at : at + rank] for piece in near], axis=-1)
                    out[chunk, o, :, place * LEAF : (place + 1) * LEAF] = (
                        far[o * cols : (o + 1) * cols] + row
                    ).astype(BF16)
        out_copy(chunk).start()

    for chunk in range(CHUNKS):
        out_copy(chunk).wait()
    for number in copies:
        run(number, "wait_send")
    for step in range(1, groups):
        root_copy(step).wait_send()
    for chunk in range(CHUNKS):
        for j in range(1, RHS):
            near_copy(chunk, j).wait_send()


def handed_on(source, target, sems):
    width = source.shape[2] // PARTS
    copies = []
    for o in range(OPS):
        for part in range(PARTS):
            piece = (o, slice(None), pl.ds(part * width, width))
            copies.append(
                pltpu.make_async_copy(
                    source.at[piece], target.at[piece], sems.at[o * PARTS + part]
                )
            )
    for copy in copies:
        copy.start()
    for copy in copies:
        copy.wait()


def per_device(
    points,
    leaf_basis,
    local_transfer,
    top_transfer,
    leaf_coupling,
    root_coupling,
    upper_coupling,
    near_blocks,
    near_offset,
    far_offset,
):
    groups = lax.axis_size("leaf")
    cols, count = points.shape
    leaves, rank, _ = leaf_basis.shape
    upper_rows = sum(groups // 2**h + 6 for h in range(1, TOPL))
    anywhere = pl.BlockSpec(memory_space=pl.ANY)
    near_shape = (RHS, leaves // 2, cols, 2 * OPS * rank)
    result = pl.pallas_call(
        functools.partial(kernel, groups),
        out_shape=jax.ShapeDtypeStruct((OPS, cols, count), BF16),
        in_specs=[anywhere] * 10,
        out_specs=anywhere,
        scratch_shapes=[
            pltpu.VMEM(points.shape, BF16),
            pltpu.SMEM((NEAR, leaves), jnp.int32),
            pltpu.SMEM((FAR, leaves), jnp.int32),
            pltpu.VMEM((CHUNKS, OPS, cols, count // CHUNKS), BF16),
            pltpu.VMEM(leaf_basis.shape, BF16),
            pltpu.VMEM(local_transfer.shape, BF16),
            pltpu.VMEM(top_transfer.shape, BF16),
            pltpu.VMEM(leaf_coupling.shape, BF16),
            pltpu.VMEM(root_coupling.shape, BF16),
            pltpu.VMEM(upper_coupling.shape, BF16),
            pltpu.VMEM(near_blocks.shape, BF16),
            pltpu.VMEM((RHS, leaves + 2 * W, cols, LEAF), BF16),
            pltpu.VMEM((leaves + 2 * W, cols, 2 * rank), BF16),
            pltpu.VMEM((leaves - 1, cols, 2 * rank), BF16),
            pltpu.VMEM((groups + 6, cols, 2 * rank), BF16),
            pltpu.VMEM((upper_rows, cols, 2 * rank), BF16),
            pltpu.VMEM((leaves, OPS * cols, rank), F32),
            pltpu.VMEM((2 * leaves, OPS * cols, rank), F32),
            pltpu.VMEM((leaves, OPS * cols, LEAF), F32),
            pltpu.VMEM(near_shape, BF16),
            pltpu.VMEM(near_shape, BF16),
            pltpu.SemaphoreType.DMA((10,)),
            pltpu.SemaphoreType.DMA((17,)),
            pltpu.SemaphoreType.DMA((17,)),
            pltpu.SemaphoreType.DMA((groups - 1,)),
            pltpu.SemaphoreType.DMA((groups - 1,)),
            pltpu.SemaphoreType.DMA((CHUNKS, RHS)),
            pltpu.SemaphoreType.DMA((CHUNKS, RHS)),
            pltpu.SemaphoreType.DMA((CHUNKS,)),
        ],
        compiler_params=pltpu.CompilerParams(
            collective_id=0, has_side_effects=True, vmem_limit_bytes=56 * 1024 * 1024
        ),
        cost_estimate=pl.CostEstimate(
            flops=900_000_000, bytes_accessed=17_000_000, transcendentals=0
        ),
    )(
        points,
        near_offset.T,
        far_offset.T,
        leaf_basis,
        local_transfer,
        top_transfer,
        leaf_coupling,
        root_coupling,
        upper_coupling,
        near_blocks,
    )
    return pl.pallas_call(
        handed_on,
        out_shape=jax.ShapeDtypeStruct(result.shape, BF16),
        in_specs=[anywhere],
        out_specs=anywhere,
        scratch_shapes=[pltpu.SemaphoreType.DMA((OPS * PARTS,))],
    )(result)


def solution(mesh):
    placed = (
        P("rhs", "leaf"),
        P("leaf", None, None),
        P("leaf", None, None, None),
        P(),
        P(None, "leaf", None, None),
        P(None, "leaf", None, None),
        P(),
        P(None, "leaf", None, "rhs", None),
        P("leaf", None),
        P("leaf", None),
    )
    return jax.shard_map(
        per_device, mesh=mesh, in_specs=placed, out_specs=P(None, "rhs", "leaf"), check_vma=False
    )
```

```python
import functools

import jax
import jax.numpy as jnp
from jax import lax
from jax.experimental import pallas as pl
from jax.experimental.pallas import tpu as pltpu
from jax.sharding import PartitionSpec as P

LEAF = 256
OPS = 3
W = 8
NEAR = 3
FAR = 5
TOPL = 3
RHS = 4
CHUNKS = 8
UNROLL = 8
MESH = pl.DeviceIdType.MESH
F32 = jnp.float32
BF16 = jnp.bfloat16


def dot_nt(a, b):
    return lax.dot_general(a, b, (((1,), (1,)), ((), ())), preferred_element_type=F32)


def dot_nn(a, b):
    return lax.dot_general(a, b, (((1,), (0,)), ((), ())), preferred_element_type=F32)


def twice(values):
    return jnp.concatenate([values, values], axis=-1).astype(BF16)


def kernel(
    groups,
    points_hbm,
    near_hbm,
    far_hbm,
    basis_hbm,
    local_hbm,
    top_hbm,
    coupling_hbm,
    root_hbm,
    upper_hbm,
    blocks_hbm,
    out_hbm,
    points,
    near_offset,
    far_offset,
    out,
    basis,
    local,
    top,
    coupling,
    root_k,
    upper_k,
    blocks,
    wide,
    coef,
    level_coef,
    roots,
    upper_coef,
    coupled,
    fields,
    far_part,
    near_send,
    near_recv,
    in_sem,
    send_sem,
    recv_sem,
    root_send,
    root_recv,
    near_ssem,
    near_rsem,
    out_sem,
):
    cols = points.shape[0]
    leaves = basis.shape[0]
    rank = basis.shape[1]
    pairs = leaves // 2
    me_l = lax.axis_index("leaf")
    me_r = lax.axis_index("rhs")
    side = me_r + 1 - 2 * (me_r % 2)
    across = (me_r + 2) % 4
    diagonal = (side + 2) % 4
    peers = (me_r, side, across, diagonal)
    has_left = me_l > 0
    has_right = me_l < groups - 1
    top_w = W + leaves

    barrier = pltpu.get_barrier_semaphore()
    for peer in peers[1:]:
        pl.semaphore_signal(barrier, inc=1, device_id=(me_l, peer), device_id_type=MESH)
    near_by = (
        (me_l - 2, me_l > 1),
        (me_l - 1, me_l > 0),
        (me_l + 1, me_l < groups - 1),
        (me_l + 2, me_l < groups - 2),
    )
    greeted = len(peers) - 1
    for neighbour, exists in near_by:
        greeted += exists.astype(jnp.int32)

        @pl.when(exists)
        def _(neighbour=neighbour):
            pl.semaphore_signal(
                barrier, inc=1, device_id=(neighbour, me_r), device_id_type=MESH
            )


    loads = [
        pltpu.make_async_copy(source, target, in_sem.at[i])
        for i, (source, target) in enumerate(
            [
                (points_hbm, points),
                (basis_hbm, basis),
                (local_hbm, local),
                (far_hbm, far_offset),
                (near_hbm, near_offset),
                (coupling_hbm, coupling),
                (blocks_hbm, blocks),
                (top_hbm, top),
                (root_hbm, root_k),
                (upper_hbm, upper_k),
            ]
        )
    ]
    for load in loads:
        load.start()

    low, high = pl.ds(0, W), pl.ds(top_w, W)
    head, tail = pl.ds(W, W), pl.ds(leaves, W)
    middle = pl.ds(2 * W, leaves - 2 * W)
    body = pl.ds(W, leaves)

    @pl.when(jnp.logical_not(has_left))
    def _():
        wide[:, 0:W] = jnp.zeros((RHS, W, cols, LEAF), BF16)
        coef[0:W] = jnp.zeros((W, cols, 2 * rank), BF16)

    @pl.when(jnp.logical_not(has_right))
    def _():
        wide[:, top_w : top_w + W] = jnp.zeros((RHS, W, cols, LEAF), BF16)
        coef[top_w : top_w + W] = jnp.zeros((W, cols, 2 * rank), BF16)

    roots[0:3] = jnp.zeros((3, cols, 2 * rank), BF16)
    roots[3 + groups : 6 + groups] = jnp.zeros((3, cols, 2 * rank), BF16)
    upper_coef[...] = jnp.zeros(upper_coef.shape, BF16)

    loads[0].wait()
    for t in range(leaves):
        wide[0, W + t] = points[:, t * LEAF : (t + 1) * LEAF]

    right = (me_l + 1) % groups
    left = (me_l + groups - 1) % groups

    def remote(number, source, target, leaf, rhs):
        return pltpu.make_async_remote_copy(
            src_ref=source,
            dst_ref=target,
            send_sem=send_sem.at[number],
            recv_sem=recv_sem.at[number],
            device_id=(leaf, rhs),
            device_id_type=MESH,
        )

    def part(slot, where):
        return wide.at[slot, where]

    copies = {
        0: (part(0, head), part(2, head), me_l, across),
        1: (part(0, tail), part(2, tail), me_l, across),
        2: (part(0, middle), part(2, middle), me_l, across),
        3: (part(0, body), part(1, body), me_l, side),
        4: (part(0, tail), part(0, low), right, me_r),
        5: (part(0, head), part(0, high), left, me_r),
        6: (part(2, tail), part(2, low), right, me_r),
        7: (part(2, head), part(2, high), left, me_r),
        8: (part(2, head), part(3, head), me_l, side),
        9: (part(2, tail), part(3, tail), me_l, side),
        10: (part(2, middle), part(3, middle), me_l, side),
        11: (part(0, low), part(1, low), me_l, side),
        12: (part(0, high), part(1, high), me_l, side),
        13: (part(2, low), part(3, low), me_l, side),
        14: (part(2, high), part(3, high), me_l, side),
        15: (coef.at[tail], coef.at[low], right, me_r),
        16: (coef.at[head], coef.at[high], left, me_r),
    }
    to_right = (4, 6, 15)
    to_left = (5, 7, 16)
    from_low = (11, 13)
    from_high = (12, 14)

    def guard(number, receiving):
        if number in to_right:
            return has_left if receiving else has_right
        if number in to_left:
            return has_right if receiving else has_left
        if number in from_low:
            return has_left
        if number in from_high:
            return has_right
        return None

    def run(number, action):
        condition = guard(number, action == "wait_recv")

        def go():
            getattr(remote(number, *copies[number]), action)()

        if condition is None:
            go()
        else:
            pl.when(condition)(go)

    def start(number):
        run(number, "start")

    def arrived(number):
        run(number, "wait_recv")

    pl.semaphore_wait(barrier, greeted)
    for number in (0, 1, 4, 5, 2, 3):
        start(number)

    first_half = lax.broadcasted_iota(jnp.int32, (cols, 2 * rank), 1) < rank

    def joined(a, b):
        return jnp.where(first_half, a.astype(F32), b.astype(F32)).astype(BF16)

    loads[1].wait()

    @pl.loop(0, leaves // UNROLL)
    def _(step):
        for u in range(UNROLL):
            t = step * UNROLL + u
            coef[W + t] = twice(dot_nt(wide[0, W + t], basis[t]))

    start(15)
    start(16)

    arrived(0)
    start(7)
    start(8)
    arrived(1)
    start(6)
    start(9)

    loads[2].wait()
    depth = leaves.bit_length() - 1
    offset = 0
    base = 0
    for height in range(depth):
        count = leaves >> height + 1
        for p in range(count):
            if height == 0:
                pair = joined(coef[W + 2 * p], coef[W + 2 * p + 1])
            else:
                pair = joined(level_coef[base + 2 * p], level_coef[base + 2 * p + 1])
            level_coef[offset + p] = twice(dot_nt(pair, local[0, offset + p]))
        base = offset
        offset += count
    roots[3 + me_l] = level_coef[leaves - 2]

    pair_count = groups // 2
    my_pair = me_l // 2
    partner = me_l + 1 - 2 * (me_l % 2)

    def root_swap():
        return pltpu.make_async_remote_copy(
            src_ref=roots.at[3 + me_l],
            dst_ref=roots.at[3 + me_l],
            send_sem=root_send.at[0, 0],
            recv_sem=root_recv.at[0, 0],
            device_id=(partner, me_r),
            device_id_type=MESH,
        )

    def relay(distance, way, action):
        sign = 1 - 2 * way
        receiving = action == "wait_recv"
        origin = my_pair - sign * (distance if receiving else distance - 1)
        target = my_pair + sign
        condition = jnp.logical_and(origin >= 0, origin < pair_count)
        if not receiving:
            condition = jnp.logical_and(
                condition, jnp.logical_and(target >= 0, target < pair_count)
            )

        @pl.when(condition)
        def _():
            rows = pl.ds(3 + 2 * origin, 2)
            copy = pltpu.make_async_remote_copy(
                src_ref=roots.at[rows],
                dst_ref=roots.at[rows],
                send_sem=root_send.at[distance, way],
                recv_sem=root_recv.at[distance, way],
                device_id=(me_l + 2 * sign, me_r),
                device_id_type=MESH,
            )
            getattr(copy, action)()

    def relay_step(distance):
        if distance == 1:
            root_swap().wait_recv()
        elif distance <= pair_count:
            for way in range(2):
                relay(distance - 1, way, "wait_recv")
        if distance < pair_count:
            for way in range(2):
                relay(distance, way, "start")

    root_swap().start()

    arrived(4)
    start(11)
    arrived(5)
    start(12)
    arrived(2)
    start(10)
    arrived(15)
    arrived(16)

    for i in (3, 4, 5):
        loads[i].wait()

    def couple_leaves(begin, end):
        @pl.loop(begin, end)
        def _(step):
            for u in range(UNROLL):
                t = step * UNROLL + u
                picked = [coef[W + t + far_offset[k, t]] for k in range(FAR)]
                pieces = [joined(picked[k], picked[k + 1]) for k in range(0, FAR - 1, 2)]
                pieces.append(picked[FAR - 1][:, :rank])
                sources = jnp.concatenate(pieces, axis=-1)
                matrix = coupling[:, t].reshape(OPS * rank, FAR * rank)
                product = dot_nt(sources, matrix)
                for o in range(OPS):
                    coupled[t, o * cols : (o + 1) * cols] = product[:, o * rank : (o + 1) * rank]

    steps = leaves // UNROLL
    couple_leaves(0, steps // 2)
    relay_step(1)
    arrived(6)
    start(13)
    arrived(7)
    start(14)
    couple_leaves(steps // 2, steps)
    relay_step(2)
    for number in (3, 8, 9, 11, 12, 10, 13, 14):
        arrived(number)

    loads[6].wait()
    chunk_pairs = pairs // CHUNKS

    def near_copy(chunk, j):
        rows = pl.ds(chunk * chunk_pairs, chunk_pairs)
        return pltpu.make_async_remote_copy(
            src_ref=near_send.at[j, rows],
            dst_ref=near_recv.at[j, rows],
            send_sem=near_ssem.at[chunk, j],
            recv_sem=near_rsem.at[chunk, j],
            device_id=(me_l, peers[j]),
            device_id_type=MESH,
        )

    def near_leaf(t):
        total = None
        for k in range(NEAR):
            left_side = wide[:, W + t + near_offset[k, t]].reshape(RHS * cols, LEAF)
            term = dot_nt(left_side, blocks[:, t, k].reshape(OPS * rank, LEAF))
            total = term if total is None else total + term
        return total

    def near_chunk(chunk):
        for step in range(chunk_pairs):
            pair = chunk * chunk_pairs + step
            first = near_leaf(2 * pair)
            second = near_leaf(2 * pair + 1)
            packed = jnp.concatenate(
                [
                    first[:, : 2 * rank],
                    second[:, : 2 * rank],
                    first[:, 2 * rank :],
                    second[:, 2 * rank :],
                ],
                axis=-1,
            ).astype(BF16)
            near_recv[0, pair] = packed[:cols]
            for j in range(1, RHS):
                near_send[j, pair] = packed[j * cols : (j + 1) * cols]

        for j in (2, 3, 1):
            near_copy(chunk, j).start()

    def top_row(height):
        return groups - groups // 2 ** (height - 1)

    def top_base(height):
        return sum(groups // 2**h + 6 for h in range(1, height))

    def top_coef(height, index):
        if height == 0:
            return roots[3 + index]
        return upper_coef[top_base(height) + 3 + index]

    def top_up():
        for height in range(1, TOPL):
            raise_level(height)

    def raise_level(height):
        for q in range(groups // 2**height):
            pair = joined(top_coef(height - 1, 2 * q), top_coef(height - 1, 2 * q + 1))
            upper_coef[top_base(height) + 3 + q] = twice(dot_nt(pair, top[top_row(height) + q]))

    def top_field(height):
        cluster = me_l // 2**height
        odd = cluster % 2
        near_by = [
            top_coef(height, cluster + s) for s in (-2 - odd, 2 - 4 * odd, 3 - odd)
        ]
        sources = jnp.concatenate([joined(near_by[0], near_by[1]), near_by[2][:, :rank]], axis=-1)
        terms = []
        for o in range(OPS):
            matrix = root_k[o, 0] if height == 0 else upper_k[o, top_row(height) + cluster]
            terms.append(dot_nt(sources, matrix))
        return jnp.concatenate(terms, axis=0)

    def top_down():
        running = top_field(TOPL - 1)
        for height in range(TOPL - 1, 0, -1):
            pushed = dot_nn(running.astype(BF16), top[top_row(height) + me_l // 2**height])
            child = (me_l // 2 ** (height - 1)) % 2
            half = jnp.where(child == 0, pushed[:, :rank], pushed[:, rank:])
            running = top_field(height - 1) + half
        fields[1] = running

    def lower_level(height):
        count = leaves >> height + 1
        offset = leaves - 2 * count
        for p in range(count):
            pushed = dot_nn(fields[count + p].astype(BF16), local[0, offset + p])
            fields[2 * (count + p)] = pushed[:, :rank]
            fields[2 * (count + p) + 1] = pushed[:, rank:]

    def lower_levels(high, low):
        for height in range(high, low - 1, -1):
            lower_level(height)

    loaded = CHUNKS // 2
    pl.loop(0, loaded // 2)(near_chunk)
    relay_step(3)
    pl.loop(loaded // 2, loaded)(near_chunk)
    for distance in range(4, max(pair_count, 3) + 1):
        relay_step(distance)
    for i in (7, 8, 9):
        loads[i].wait()
    stages = (
        top_up,
        top_down,
        functools.partial(lower_levels, depth - 1, 1),
        functools.partial(lower_levels, 0, 0),
    )
    for chunk, stage in zip(range(loaded, CHUNKS), stages):
        stage()
        near_chunk(chunk)

    for t in range(leaves):
        leaf_field = (fields[leaves + t] + coupled[t]).astype(BF16)
        far_part[t] = dot_nn(leaf_field, basis[t])

    slots = (me_r, side, across, diagonal)
    chunk_points = 2 * chunk_pairs * LEAF

    def out_copy(chunk):
        where = pl.ds(pl.multiple_of(chunk * chunk_points, chunk_points), chunk_points)
        return pltpu.make_async_copy(
            out.at[chunk], out_hbm.at[:, :, where], out_sem.at[chunk]
        )

    @pl.loop(0, CHUNKS)
    def _(chunk):
        for j in range(1, RHS):
            near_copy(chunk, j).wait_recv()
        for step in range(chunk_pairs):
            pair = chunk * chunk_pairs + step
            near = [near_recv[slots[r], pair].astype(F32) for r in range(RHS)]
            for e in range(2):
                place = 2 * step + e
                far = far_part[2 * pair + e]
                for o in range(OPS):
                    at = (2 * e + o if o < 2 else 4 + e) * rank
                    row = jnp.concatenate([piece[:, at : at + rank] for piece in near], axis=-1)
                    out[chunk, o, :, place * LEAF : (place + 1) * LEAF] = (
                        far[o * cols : (o + 1) * cols] + row
                    ).astype(BF16)
        out_copy(chunk).start()

    for chunk in range(CHUNKS):
        out_copy(chunk).wait()
    for number in copies:
        run(number, "wait_send")
    root_swap().wait_send()
    for distance in range(1, pair_count):
        for way in range(2):
            relay(distance, way, "wait_send")
    for chunk in range(CHUNKS):
        for j in range(1, RHS):
            near_copy(chunk, j).wait_send()


def handed_on(source, target, held, sems):
    ins = []
    outs = []
    for o in range(OPS):
        ins.append(pltpu.make_async_copy(source.at[o], held.at[o], sems.at[0, o]))
        outs.append(pltpu.make_async_copy(held.at[o], target.at[o], sems.at[1, o]))
    for copy in ins:
        copy.start()
    for into, onward in zip(ins, outs):
        into.wait()
        onward.start()
    for copy in outs:
        copy.wait()


def per_device(
    points,
    leaf_basis,
    local_transfer,
    top_transfer,
    leaf_coupling,
    root_coupling,
    upper_coupling,
    near_blocks,
    near_offset,
    far_offset,
):
    groups = lax.axis_size("leaf")
    cols, count = points.shape
    leaves, rank, _ = leaf_basis.shape
    upper_rows = sum(groups // 2**h + 6 for h in range(1, TOPL))
    anywhere = pl.BlockSpec(memory_space=pl.ANY)
    near_shape = (RHS, leaves // 2, cols, 2 * OPS * rank)
    result = pl.pallas_call(
        functools.partial(kernel, groups),
        out_shape=jax.ShapeDtypeStruct((OPS, cols, count), BF16),
        in_specs=[anywhere] * 10,
        out_specs=anywhere,
        scratch_shapes=[
            pltpu.VMEM(points.shape, BF16),
            pltpu.SMEM((NEAR, leaves), jnp.int32),
            pltpu.SMEM((FAR, leaves), jnp.int32),
            pltpu.VMEM((CHUNKS, OPS, cols, count // CHUNKS), BF16),
            pltpu.VMEM(leaf_basis.shape, BF16),
            pltpu.VMEM(local_transfer.shape, BF16),
            pltpu.VMEM(top_transfer.shape, BF16),
            pltpu.VMEM(leaf_coupling.shape, BF16),
            pltpu.VMEM(root_coupling.shape, BF16),
            pltpu.VMEM(upper_coupling.shape, BF16),
            pltpu.VMEM(near_blocks.shape, BF16),
            pltpu.VMEM((RHS, leaves + 2 * W, cols, LEAF), BF16),
            pltpu.VMEM((leaves + 2 * W, cols, 2 * rank), BF16),
            pltpu.VMEM((leaves - 1, cols, 2 * rank), BF16),
            pltpu.VMEM((groups + 6, cols, 2 * rank), BF16),
            pltpu.VMEM((upper_rows, cols, 2 * rank), BF16),
            pltpu.VMEM((leaves, OPS * cols, rank), F32),
            pltpu.VMEM((2 * leaves, OPS * cols, rank), F32),
            pltpu.VMEM((leaves, OPS * cols, LEAF), F32),
            pltpu.VMEM(near_shape, BF16),
            pltpu.VMEM(near_shape, BF16),
            pltpu.SemaphoreType.DMA((10,)),
            pltpu.SemaphoreType.DMA((17,)),
            pltpu.SemaphoreType.DMA((17,)),
            pltpu.SemaphoreType.DMA((groups // 2, 2)),
            pltpu.SemaphoreType.DMA((groups // 2, 2)),
            pltpu.SemaphoreType.DMA((CHUNKS, RHS)),
            pltpu.SemaphoreType.DMA((CHUNKS, RHS)),
            pltpu.SemaphoreType.DMA((CHUNKS,)),
        ],
        compiler_params=pltpu.CompilerParams(
            collective_id=0, has_side_effects=True, vmem_limit_bytes=56 * 1024 * 1024
        ),
        cost_estimate=pl.CostEstimate(
            flops=900_000_000, bytes_accessed=17_000_000, transcendentals=0
        ),
    )(
        points,
        near_offset.T,
        far_offset.T,
        leaf_basis,
        local_transfer,
        top_transfer,
        leaf_coupling,
        root_coupling,
        upper_coupling,
        near_blocks,
    )
    return pl.pallas_call(
        handed_on,
        out_shape=jax.ShapeDtypeStruct(result.shape, BF16),
        in_specs=[anywhere],
        out_specs=anywhere,
        scratch_shapes=[
            pltpu.VMEM(result.shape, BF16),
            pltpu.SemaphoreType.DMA((2, OPS)),
        ],
    )(result)


def solution(mesh):
    placed = (
        P("rhs", "leaf"),
        P("leaf", None, None),
        P("leaf", None, None, None),
        P(),
        P(None, "leaf", None, None),
        P(None, "leaf", None, None),
        P(),
        P(None, "leaf", None, "rhs", None),
        P("leaf", None),
        P("leaf", None),
    )
    return jax.shard_map(
        per_device, mesh=mesh, in_specs=placed, out_specs=P(None, "rhs", "leaf"), check_vma=False
    )
```

```python
import functools

import jax
import jax.numpy as jnp
from jax import lax
from jax.experimental import pallas as pl
from jax.experimental.pallas import tpu as pltpu
from jax.sharding import PartitionSpec as P

LEAF = 256
OPS = 3
W = 8
NEAR = 3
FAR = 5
TOPL = 3
RHS = 4
CHUNKS = 4
UNROLL = 8
MESH = pl.DeviceIdType.MESH
F32 = jnp.float32
BF16 = jnp.bfloat16


def dot_nt(a, b):
    return lax.dot_general(a, b, (((1,), (1,)), ((), ())), preferred_element_type=F32)


def dot_nn(a, b):
    return lax.dot_general(a, b, (((1,), (0,)), ((), ())), preferred_element_type=F32)


def twice(values):
    return jnp.concatenate([values, values], axis=-1).astype(BF16)


def kernel(
    groups,
    points_hbm,
    near_hbm,
    far_hbm,
    basis_hbm,
    local_hbm,
    top_hbm,
    coupling_hbm,
    root_hbm,
    upper_hbm,
    blocks_hbm,
    out_hbm,
    points,
    near_offset,
    far_offset,
    out,
    basis,
    local,
    top,
    coupling,
    root_k,
    upper_k,
    blocks,
    wide,
    coef,
    level_coef,
    roots,
    upper_coef,
    coupled,
    fields,
    far_part,
    near_send,
    near_recv,
    in_sem,
    send_sem,
    recv_sem,
    root_send,
    root_recv,
    near_ssem,
    near_rsem,
    out_sem,
):
    cols = points.shape[0]
    leaves = basis.shape[0]
    rank = basis.shape[1]
    pairs = leaves // 2
    me_l = lax.axis_index("leaf")
    me_r = lax.axis_index("rhs")
    side = me_r + 1 - 2 * (me_r % 2)
    across = (me_r + 2) % 4
    diagonal = (side + 2) % 4
    peers = (me_r, side, across, diagonal)
    has_left = me_l > 0
    has_right = me_l < groups - 1
    top_w = W + leaves

    barrier = pltpu.get_barrier_semaphore()
    for peer in peers[1:]:
        pl.semaphore_signal(barrier, inc=1, device_id=(me_l, peer), device_id_type=MESH)
    for step in range(1, groups):
        pl.semaphore_signal(
            barrier, inc=1, device_id=((me_l + step) % groups, me_r), device_id_type=MESH
        )

    loads = [
        pltpu.make_async_copy(source, target, in_sem.at[i])
        for i, (source, target) in enumerate(
            [
                (points_hbm, points),
                (basis_hbm, basis),
                (local_hbm, local),
                (far_hbm, far_offset),
                (near_hbm, near_offset),
                (coupling_hbm, coupling),
                (blocks_hbm, blocks),
                (top_hbm, top),
                (root_hbm, root_k),
                (upper_hbm, upper_k),
            ]
        )
    ]
    for load in loads:
        load.start()

    low, high = pl.ds(0, W), pl.ds(top_w, W)
    head, tail = pl.ds(W, W), pl.ds(leaves, W)
    middle = pl.ds(2 * W, leaves - 2 * W)
    body = pl.ds(W, leaves)

    @pl.when(jnp.logical_not(has_left))
    def _():
        wide[:, 0:W] = jnp.zeros((RHS, W, cols, LEAF), BF16)
        coef[0:W] = jnp.zeros((W, cols, 2 * rank), BF16)

    @pl.when(jnp.logical_not(has_right))
    def _():
        wide[:, top_w : top_w + W] = jnp.zeros((RHS, W, cols, LEAF), BF16)
        coef[top_w : top_w + W] = jnp.zeros((W, cols, 2 * rank), BF16)

    roots[0:3] = jnp.zeros((3, cols, 2 * rank), BF16)
    roots[3 + groups : 6 + groups] = jnp.zeros((3, cols, 2 * rank), BF16)
    upper_coef[...] = jnp.zeros(upper_coef.shape, BF16)

    loads[0].wait()
    for t in range(leaves):
        wide[0, W + t] = points[:, t * LEAF : (t + 1) * LEAF]

    right = (me_l + 1) % groups
    left = (me_l + groups - 1) % groups

    def remote(number, source, target, leaf, rhs):
        return pltpu.make_async_remote_copy(
            src_ref=source,
            dst_ref=target,
            send_sem=send_sem.at[number],
            recv_sem=recv_sem.at[number],
            device_id=(leaf, rhs),
            device_id_type=MESH,
        )

    def part(slot, where):
        return wide.at[slot, where]

    copies = {
        0: (part(0, head), part(2, head), me_l, across),
        1: (part(0, tail), part(2, tail), me_l, across),
        2: (part(0, middle), part(2, middle), me_l, across),
        3: (part(0, body), part(1, body), me_l, side),
        4: (part(0, tail), part(0, low), right, me_r),
        5: (part(0, head), part(0, high), left, me_r),
        6: (part(2, tail), part(2, low), right, me_r),
        7: (part(2, head), part(2, high), left, me_r),
        8: (part(2, head), part(3, head), me_l, side),
        9: (part(2, tail), part(3, tail), me_l, side),
        10: (part(2, middle), part(3, middle), me_l, side),
        11: (part(0, low), part(1, low), me_l, side),
        12: (part(0, high), part(1, high), me_l, side),
        13: (part(2, low), part(3, low), me_l, side),
        14: (part(2, high), part(3, high), me_l, side),
        15: (coef.at[tail], coef.at[low], right, me_r),
        16: (coef.at[head], coef.at[high], left, me_r),
    }
    to_right = (4, 6, 15)
    to_left = (5, 7, 16)
    from_low = (11, 13)
    from_high = (12, 14)

    def guard(number, receiving):
        if number in to_right:
            return has_left if receiving else has_right
        if number in to_left:
            return has_right if receiving else has_left
        if number in from_low:
            return has_left
        if number in from_high:
            return has_right
        return None

    def run(number, action):
        condition = guard(number, action == "wait_recv")

        def go():
            getattr(remote(number, *copies[number]), action)()

        if condition is None:
            go()
        else:
            pl.when(condition)(go)

    def start(number):
        run(number, "start")

    def arrived(number):
        run(number, "wait_recv")

    pl.semaphore_wait(barrier, len(peers) - 1 + groups - 1)
    for number in (0, 1, 4, 5, 2, 3):
        start(number)

    first_half = lax.broadcasted_iota(jnp.int32, (cols, 2 * rank), 1) < rank

    def joined(a, b):
        return jnp.where(first_half, a.astype(F32), b.astype(F32)).astype(BF16)

    loads[1].wait()

    @pl.loop(0, leaves // UNROLL)
    def _(step):
        for u in range(UNROLL):
            t = step * UNROLL + u
            coef[W + t] = twice(dot_nt(wide[0, W + t], basis[t]))

    start(15)
    start(16)

    arrived(0)
    start(7)
    start(8)
    arrived(1)
    start(6)
    start(9)

    loads[2].wait()
    depth = leaves.bit_length() - 1
    offset = 0
    base = 0
    for height in range(depth):
        count = leaves >> height + 1
        for p in range(count):
            if height == 0:
                pair = joined(coef[W + 2 * p], coef[W + 2 * p + 1])
            else:
                pair = joined(level_coef[base + 2 * p], level_coef[base + 2 * p + 1])
            level_coef[offset + p] = twice(dot_nt(pair, local[0, offset + p]))
        base = offset
        offset += count
    roots[3 + me_l] = level_coef[leaves - 2]

    def root_copy(step):
        return pltpu.make_async_remote_copy(
            src_ref=roots.at[3 + me_l],
            dst_ref=roots.at[3 + me_l],
            send_sem=root_send.at[step - 1],
            recv_sem=root_recv.at[step - 1],
            device_id=((me_l + step) % groups, me_r),
            device_id_type=MESH,
        )

    for step in range(1, groups):
        root_copy(step).start()

    arrived(4)
    start(11)
    arrived(5)
    start(12)
    arrived(2)
    start(10)
    arrived(15)
    arrived(16)

    for i in (3, 4, 5):
        loads[i].wait()

    def couple_leaves(begin, end):
        @pl.loop(begin, end)
        def _(step):
            for u in range(UNROLL):
                t = step * UNROLL + u
                picked = [coef[W + t + far_offset[k, t]] for k in range(FAR)]
                pieces = [joined(picked[k], picked[k + 1]) for k in range(0, FAR - 1, 2)]
                pieces.append(picked[FAR - 1][:, :rank])
                sources = jnp.concatenate(pieces, axis=-1)
                matrix = coupling[:, t].reshape(OPS * rank, FAR * rank)
                product = dot_nt(sources, matrix)
                for o in range(OPS):
                    coupled[t, o * cols : (o + 1) * cols] = product[:, o * rank : (o + 1) * rank]

    steps = leaves // UNROLL
    couple_leaves(0, steps // 2)
    arrived(6)
    start(13)
    arrived(7)
    start(14)
    couple_leaves(steps // 2, steps)
    for number in (3, 8, 9, 11, 12, 10, 13, 14):
        arrived(number)

    loads[6].wait()
    chunk_pairs = pairs // CHUNKS

    def near_copy(chunk, j):
        rows = pl.ds(chunk * chunk_pairs, chunk_pairs)
        return pltpu.make_async_remote_copy(
            src_ref=near_send.at[j, rows],
            dst_ref=near_recv.at[j, rows],
            send_sem=near_ssem.at[chunk, j],
            recv_sem=near_rsem.at[chunk, j],
            device_id=(me_l, peers[j]),
            device_id_type=MESH,
        )

    def near_leaf(t):
        sources = [
            wide[:, W + t + near_offset[k, t]].reshape(RHS * cols, LEAF) for k in range(NEAR)
        ]
        matrices = [blocks[:, t, k].reshape(OPS * rank, LEAF) for k in range(NEAR)]
        return dot_nt(jnp.concatenate(sources, axis=-1), jnp.concatenate(matrices, axis=-1))

    @pl.loop(0, CHUNKS)
    def _(chunk):
        for step in range(chunk_pairs):
            pair = chunk * chunk_pairs + step
            first = near_leaf(2 * pair)
            second = near_leaf(2 * pair + 1)
            packed = jnp.concatenate(
                [
                    first[:, : 2 * rank],
                    second[:, : 2 * rank],
                    first[:, 2 * rank :],
                    second[:, 2 * rank :],
                ],
                axis=-1,
            ).astype(BF16)
            near_recv[0, pair] = packed[:cols]
            for j in range(1, RHS):
                near_send[j, pair] = packed[j * cols : (j + 1) * cols]

        for j in (2, 3, 1):
            near_copy(chunk, j).start()

    for step in range(1, groups):
        root_copy(step).wait_recv()
    for i in (7, 8, 9):
        loads[i].wait()

    def top_row(height):
        return groups - groups // 2 ** (height - 1)

    def top_base(height):
        return sum(groups // 2**h + 6 for h in range(1, height))

    def top_coef(height, index):
        if height == 0:
            return roots[3 + index]
        return upper_coef[top_base(height) + 3 + index]

    for height in range(1, TOPL):
        for q in range(groups // 2**height):
            pair = joined(top_coef(height - 1, 2 * q), top_coef(height - 1, 2 * q + 1))
            upper_coef[top_base(height) + 3 + q] = twice(dot_nt(pair, top[top_row(height) + q]))

    def top_field(height):
        cluster = me_l // 2**height
        odd = cluster % 2
        near_by = [
            top_coef(height, cluster + s) for s in (-2 - odd, 2 - 4 * odd, 3 - odd)
        ]
        sources = jnp.concatenate([joined(near_by[0], near_by[1]), near_by[2][:, :rank]], axis=-1)
        terms = []
        for o in range(OPS):
            matrix = root_k[o, 0] if height == 0 else upper_k[o, top_row(height) + cluster]
            terms.append(dot_nt(sources, matrix))
        return jnp.concatenate(terms, axis=0)

    running = top_field(TOPL - 1)
    for height in range(TOPL - 1, 0, -1):
        pushed = dot_nn(running.astype(BF16), top[top_row(height) + me_l // 2**height])
        child = (me_l // 2 ** (height - 1)) % 2
        half = jnp.where(child == 0, pushed[:, :rank], pushed[:, rank:])
        running = top_field(height - 1) + half

    fields[1] = running
    for height in reversed(range(depth)):
        count = leaves >> height + 1
        offset = leaves - 2 * count
        for p in range(count):
            pushed = dot_nn(fields[count + p].astype(BF16), local[0, offset + p])
            fields[2 * (count + p)] = pushed[:, :rank]
            fields[2 * (count + p) + 1] = pushed[:, rank:]

    for t in range(leaves):
        leaf_field = (fields[leaves + t] + coupled[t]).astype(BF16)
        far_part[t] = dot_nn(leaf_field, basis[t])

    slots = (me_r, side, across, diagonal)
    chunk_points = 2 * chunk_pairs * LEAF

    def out_copy(chunk):
        where = pl.ds(pl.multiple_of(chunk * chunk_points, chunk_points), chunk_points)
        return pltpu.make_async_copy(
            out.at[chunk], out_hbm.at[:, :, where], out_sem.at[chunk]
        )

    @pl.loop(0, CHUNKS)
    def _(chunk):
        for j in range(1, RHS):
            near_copy(chunk, j).wait_recv()
        for step in range(chunk_pairs):
            pair = chunk * chunk_pairs + step
            near = [near_recv[slots[r], pair].astype(F32) for r in range(RHS)]
            for e in range(2):
                place = 2 * step + e
                far = far_part[2 * pair + e]
                for o in range(OPS):
                    at = (2 * e + o if o < 2 else 4 + e) * rank
                    row = jnp.concatenate([piece[:, at : at + rank] for piece in near], axis=-1)
                    out[chunk, o, :, place * LEAF : (place + 1) * LEAF] = (
                        far[o * cols : (o + 1) * cols] + row
                    ).astype(BF16)
        out_copy(chunk).start()

    for chunk in range(CHUNKS):
        out_copy(chunk).wait()
    for number in copies:
        run(number, "wait_send")
    for step in range(1, groups):
        root_copy(step).wait_send()
    for chunk in range(CHUNKS):
        for j in range(1, RHS):
            near_copy(chunk, j).wait_send()


def per_device(
    points,
    leaf_basis,
    local_transfer,
    top_transfer,
    leaf_coupling,
    root_coupling,
    upper_coupling,
    near_blocks,
    near_offset,
    far_offset,
):
    groups = lax.axis_size("leaf")
    cols, count = points.shape
    leaves, rank, _ = leaf_basis.shape
    upper_rows = sum(groups // 2**h + 6 for h in range(1, TOPL))
    anywhere = pl.BlockSpec(memory_space=pl.ANY)
    near_shape = (RHS, leaves // 2, cols, 2 * OPS * rank)
    return pl.pallas_call(
        functools.partial(kernel, groups),
        out_shape=jax.ShapeDtypeStruct((OPS, cols, count), BF16),
        in_specs=[anywhere] * 10,
        out_specs=anywhere,
        scratch_shapes=[
            pltpu.VMEM(points.shape, BF16),
            pltpu.SMEM((NEAR, leaves), jnp.int32),
            pltpu.SMEM((FAR, leaves), jnp.int32),
            pltpu.VMEM((CHUNKS, OPS, cols, count // CHUNKS), BF16),
            pltpu.VMEM(leaf_basis.shape, BF16),
            pltpu.VMEM(local_transfer.shape, BF16),
            pltpu.VMEM(top_transfer.shape, BF16),
            pltpu.VMEM(leaf_coupling.shape, BF16),
            pltpu.VMEM(root_coupling.shape, BF16),
            pltpu.VMEM(upper_coupling.shape, BF16),
            pltpu.VMEM(near_blocks.shape, BF16),
            pltpu.VMEM((RHS, leaves + 2 * W, cols, LEAF), BF16),
            pltpu.VMEM((leaves + 2 * W, cols, 2 * rank), BF16),
            pltpu.VMEM((leaves - 1, cols, 2 * rank), BF16),
            pltpu.VMEM((groups + 6, cols, 2 * rank), BF16),
            pltpu.VMEM((upper_rows, cols, 2 * rank), BF16),
            pltpu.VMEM((leaves, OPS * cols, rank), F32),
            pltpu.VMEM((2 * leaves, OPS * cols, rank), F32),
            pltpu.VMEM((leaves, OPS * cols, LEAF), F32),
            pltpu.VMEM(near_shape, BF16),
            pltpu.VMEM(near_shape, BF16),
            pltpu.SemaphoreType.DMA((10,)),
            pltpu.SemaphoreType.DMA((17,)),
            pltpu.SemaphoreType.DMA((17,)),
            pltpu.SemaphoreType.DMA((groups - 1,)),
            pltpu.SemaphoreType.DMA((groups - 1,)),
            pltpu.SemaphoreType.DMA((CHUNKS, RHS)),
            pltpu.SemaphoreType.DMA((CHUNKS, RHS)),
            pltpu.SemaphoreType.DMA((CHUNKS,)),
        ],
        compiler_params=pltpu.CompilerParams(
            collective_id=0, has_side_effects=True, vmem_limit_bytes=56 * 1024 * 1024
        ),
        cost_estimate=pl.CostEstimate(
            flops=900_000_000, bytes_accessed=17_000_000, transcendentals=0
        ),
    )(
        points,
        near_offset.T,
        far_offset.T,
        leaf_basis,
        local_transfer,
        top_transfer,
        leaf_coupling,
        root_coupling,
        upper_coupling,
        near_blocks,
    )


def solution(mesh):
    placed = (
        P("rhs", "leaf"),
        P("leaf", None, None),
        P("leaf", None, None, None),
        P(),
        P(None, "leaf", None, None),
        P(None, "leaf", None, None),
        P(),
        P(None, "leaf", None, "rhs", None),
        P("leaf", None),
        P("leaf", None),
    )
    return jax.shard_map(
        per_device, mesh=mesh, in_specs=placed, out_specs=P(None, "rhs", "leaf"), check_vma=False
    )
```
